256 devices in a mesh: qrow: 8 (over x, z_lo), kcol: 32 (over y, z_hi, core).
Axes of the slice: x: 4, y: 4, z: 8 (z_hi: 4, z_lo: 2; z = z_hi * 2 + z_lo), core: 2. Of those that a mesh axis runs over, the one named last changes fastest.
Arguments:
- queries: bfloat16 [256, 2048], P(('qrow', 'kcol')), may hold values from -96 to 96, as said below
- key_maps: bfloat16 [65536, 2048], P(('qrow', 'kcol')), may hold values from -4.1 to 4.1, as said below
- values: bfloat16 [65536, 2048], P(('qrow', 'kcol')), may hold values from -24 to 24
- lambdas: float32 [8], replicated, may hold values from 0.2 to 0.8
- norm_gain: float32 [2048], replicated, may hold values from 0.1 to 1.9
Outputs:
- attended: bfloat16 [256, 2048], P(('qrow', 'kcol'))
The draws below stay inside these ranges and needn't reach their ends.
Inputs may be any that keep to these rules, and one draw needn't show every extreme that they name: `queries`: query features of order one in most rows. `key_maps`: key features of order one.
All inputs are finite; a program needn't handle non-finite values.
Results may differ from the reference program's by a relative error of at most 0.014.
Values may be sent and summed in bfloat16 or wider, within the bound.
No kernel may reach another device: no remote copies, remote signals or barrier semaphores. Data moves between devices by JAX's collectives and lax.ppermute only.
A program may use at most 64 MiB of HBM per device.

```python
import math
import jax
import jax.numpy as jnp
from jax import lax

HEADS = 8
HD = 128
VD = 256
Q = 256
CTX = 65536
N_QROW = 8


def shared_keys(key):
    return jnp.clip(jax.random.normal(key, (CTX, 2 * HEADS * HD), jnp.float32), -4.0, 4.0)


def draw_key_maps(key, part):
    base = shared_keys(key)
    return base.astype(jnp.bfloat16)


def draw_queries(key, part):
    key = jax.random.fold_in(key, 2)
    result = jnp.clip(1.6 * jax.random.normal(key, (Q, 2 * HEADS * HD), jnp.float32), -6.4, 6.4)
    return result.astype(jnp.bfloat16)


def steps_of(key, dims, cuts, least, high):
    factor_of, own = 1.0, jax.random.fold_in(key, 6)
    for position, parts in cuts:
        draws = jnp.exp(jax.random.uniform(jax.random.fold_in(own, position), (parts,), jnp.float32, least / len(cuts), high / len(cuts)))
        factor_of = factor_of * jnp.repeat(draws, dims[position] // parts).reshape([-1 if axis == position else 1 for axis in range(len(dims))])
    return factor_of


def normal_values(stream_key, shape, width, reach, shards=(), held_as=jnp.bfloat16):
    drawn = width * jax.random.normal(stream_key, shape, jnp.float32)
    if shards:
        drawn = drawn * steps_of(stream_key, shape, shards, -0.22, 0.18)
    return jnp.clip(drawn, -reach, reach).astype(held_as)


def setup_inputs(seed: int = 0) -> dict:
    seeds = jax.random.split(jax.random.key(seed), 6)
    return {
        "queries": draw_queries(jax.random.fold_in(seeds[5], 71), 0),
        "key_maps": draw_key_maps(jax.random.fold_in(seeds[5], 71), 0),
        "values": normal_values(seeds[2], (CTX, HEADS * VD), 4.0, 24.0, ((0, 256),)),
        "lambdas": jnp.clip(jax.random.uniform(seeds[3], (HEADS,), jnp.float32, 0.2, 0.8), 0.2, 0.8),
        "norm_gain": jnp.clip(1.0 + 0.18 * jax.random.normal(seeds[4], (HEADS * VD,), jnp.float32), 0.1, 1.9),
    }


def reference(queries, key_maps, values, lambdas, norm_gain):
    scaling = 1.0 / math.sqrt(HD)
    per_block = Q // N_QROW
    block_count = Q // per_block
    key_heads = key_maps.reshape(CTX, HEADS, 2, HD).transpose(1, 2, 0, 3)
    value_heads = values.reshape(CTX, HEADS, VD).transpose(1, 0, 2)
    query_blocks = queries.reshape(block_count, per_block, HEADS, 2, HD).transpose(0, 2, 3, 1, 4)
    key_pos = jnp.arange(CTX, dtype=jnp.int32)
    starts = (jnp.arange(block_count, dtype=jnp.int32) * per_block).astype(jnp.int32)

    def one_block(inputs):
        query_heads, first = inputs
        query_pos = (CTX - Q + first + jnp.arange(per_block, dtype=jnp.int32)).astype(jnp.int32)
        visible = key_pos[None, :] <= query_pos[:, None]

        def one_head(head_inputs):
            query_pair, key_pair, value_rows, weight_two = head_inputs
            outputs = []
            for map_side in range(2):
                score = jnp.dot(query_pair[map_side], key_pair[map_side].T, preferred_element_type=jnp.float32) * scaling
                score = jnp.where(visible, score, -1e+30)
                largest = lax.optimization_barrier(jnp.max(score, axis=1))
                expo = jnp.where(visible, jnp.exp(score - largest[:, None]), 0.0)
                total = lax.optimization_barrier(jnp.sum(expo, axis=1))
                summed = jnp.dot(expo.astype(jnp.bfloat16), value_rows, preferred_element_type=jnp.float32)
                outputs.append(summed / total[:, None])
            return outputs[0] - weight_two * outputs[1]
        return lax.map(one_head, (query_heads, key_heads, value_heads, lambdas))
    diffs = lax.map(one_block, (query_blocks, starts))
    diffs = diffs.transpose(0, 2, 1, 3).reshape(Q, HEADS, VD)
    meansq = lax.optimization_barrier(jnp.mean(diffs * diffs, axis=-1, keepdims=True))
    normed = diffs / jnp.sqrt(meansq + 1e-05) * norm_gain.reshape(HEADS, VD)
    return normed.reshape(Q, HEADS * VD).astype(jnp.bfloat16)
```

```python
import functools
import math

import jax
import jax.numpy as jnp
from jax import lax
from jax.experimental import pallas as pl
from jax.experimental.pallas import tpu as pltpu
from jax.sharding import Mesh, PartitionSpec as P

HEADS = 8
MAPS = 16
HD = 128
VD = 256
KEYS = 256
DEVICES = 256
CHIPS = 128
PLANE = 16
COLUMN = 8
SUMS = MAPS * VD
WIDE = SUMS + 128
NEG = -1e30
AXES = ("x", "z_lo", "y", "z_hi", "core")
BF16 = jnp.bfloat16
F32 = jnp.float32


def attend(place_ref, q_ref, ka_ref, va_ref, kb_ref, vb_ref, out_ref, stats_ref):
    head = pl.program_id(0)
    place = place_ref[0]
    core = place % 2
    row = lax.broadcasted_iota(jnp.int32, (CHIPS, KEYS), 0)
    device = (row // 32) * 64 + ((row // 4) % 2) * 32 + ((row // 8) % 4) * 8 + (row % 4) * 2 + core
    ahead = device - lax.broadcasted_iota(jnp.int32, (CHIPS, KEYS), 1) + (DEVICES - 1) * KEYS
    seen_a = ahead >= place * KEYS
    seen_b = ahead >= (place + 1 - 2 * core) * KEYS
    scaling = math.log2(math.e) / math.sqrt(HD)
    lane = lax.broadcasted_iota(jnp.int32, (CHIPS, 128), 1)
    trans = (((1,), (1,)), ((), ()))

    @pl.when(head == 0)
    def _():
        stats_ref[...] = jnp.zeros_like(stats_ref)

    stats = stats_ref[...]
    for side in range(2):
        cols = slice(side * HD, (side + 1) * HD)
        q = q_ref[:, cols]
        sa = lax.dot_general(q, ka_ref[:, cols], trans, preferred_element_type=F32) * scaling
        sb = lax.dot_general(q, kb_ref[:, cols], trans, preferred_element_type=F32) * scaling
        sa = jnp.where(seen_a, sa, NEG)
        sb = jnp.where(seen_b, sb, NEG)
        top = jnp.max(jnp.maximum(sa, sb), axis=1, keepdims=True).astype(BF16).astype(F32)
        ea = jnp.exp2(sa - top)
        eb = jnp.exp2(sb - top)
        total = jnp.sum(ea + eb, axis=1, keepdims=True)
        acc = jnp.dot(ea.astype(BF16), va_ref[...], preferred_element_type=F32)
        acc += jnp.dot(eb.astype(BF16), vb_ref[...], preferred_element_type=F32)
        index = head * 2 + side
        out_ref[:, pl.ds(pl.multiple_of(index * VD, VD), VD)] = acc.astype(BF16)
        high = total.astype(BF16).astype(F32)
        stats = jnp.where(lane == index, top, stats)
        stats = jnp.where(lane == index + MAPS, high, stats)
        stats = jnp.where(lane == index + 2 * MAPS, total - high, stats)
    stats_ref[...] = stats

    @pl.when(head == HEADS - 1)
    def _():
        out_ref[:, SUMS:] = stats.astype(BF16)


def merge_plane(in_ref, out_ref):
    stats = in_ref[:, SUMS:].astype(F32)
    total = pltpu.roll(stats, 128 - MAPS, 1) + pltpu.roll(stats, 128 - 2 * MAPS, 1)
    stats = stats.reshape(PLANE, COLUMN, 128)
    total = total.reshape(PLANE, COLUMN, 128)
    top = jnp.max(stats, axis=0)
    weight = jnp.exp2(stats - top[None])
    total = jnp.sum(weight * total, axis=0)
    lane = lax.broadcasted_iota(jnp.int32, (COLUMN, 128), 1)
    out_ref[:, SUMS:] = jnp.where(lane < MAPS, top, pltpu.roll(total, MAPS, 1))
    for index in range(MAPS):
        cols = slice(index * VD, (index + 1) * VD)
        part = in_ref[:, cols].astype(F32).reshape(PLANE, COLUMN, VD)
        out_ref[:, cols] = jnp.sum(part * weight[:, :, index : index + 1], axis=0)


def merge_column(lam_ref, in_ref, gain_ref, out_ref):
    stats = in_ref[:, SUMS:]
    total = pltpu.roll(stats, 128 - MAPS, 1)
    top = jnp.max(stats, axis=0, keepdims=True)
    weight = jnp.exp2(stats - top)
    lane = lax.broadcasted_iota(jnp.int32, (COLUMN, 128), 1)
    total = jnp.where(lane < MAPS, jnp.sum(weight * total, axis=0, keepdims=True), 1.0)
    weight = weight / total
    for head in range(HEADS):
        outs = []
        for index in (2 * head, 2 * head + 1):
            part = in_ref[:, index * VD : (index + 1) * VD]
            outs.append(jnp.sum(part * weight[:, index : index + 1], axis=0, keepdims=True))
        diff = outs[0] - lam_ref[head] * outs[1]
        meansq = jnp.mean(diff * diff, axis=1, keepdims=True)
        cols = slice(head * VD, (head + 1) * VD)
        out_ref[:, cols] = (diff / jnp.sqrt(meansq + 1e-5) * gain_ref[:, cols]).astype(BF16)


def shards(queries, key_maps, values, lambdas, norm_gain):
    swap = [(0, 1), (1, 0)]
    key_other = lax.ppermute(key_maps, "core", swap)
    value_other = lax.ppermute(values, "core", swap)
    place = lax.axis_index(AXES).astype(jnp.int32).reshape(1)

    spread = jnp.broadcast_to(queries.reshape(1, MAPS, HD), (COLUMN, MAPS, HD))
    column = lax.all_to_all(spread, ("z_lo", "z_hi"), 0, 0, tiled=True)
    column = column.reshape(1, COLUMN, MAPS * HD)
    spread = jnp.broadcast_to(column, (PLANE, COLUMN, MAPS * HD))
    q_all = lax.all_to_all(spread, ("x", "y"), 0, 0, tiled=True).reshape(CHIPS, MAPS * HD)

    per_head = pl.BlockSpec((KEYS, 2 * HD), lambda h: (0, h))
    partial = pl.pallas_call(
        attend,
        grid=(HEADS,),
        in_specs=[
            pl.BlockSpec(memory_space=pltpu.SMEM),
            pl.BlockSpec((CHIPS, 2 * HD), lambda h: (0, h)),
            per_head,
            per_head,
            per_head,
            per_head,
        ],
        out_specs=pl.BlockSpec((CHIPS, WIDE), lambda h: (0, 0)),
        out_shape=jax.ShapeDtypeStruct((CHIPS, WIDE), BF16),
        scratch_shapes=[pltpu.VMEM((CHIPS, 128), F32)],
        name="attend",
    )(place, q_all, key_maps, values, key_other, value_other)

    partial = partial.reshape(PLANE, COLUMN, WIDE)
    partial = lax.all_to_all(partial, ("x", "y"), 0, 0, tiled=True)
    merged = pl.pallas_call(
        merge_plane,
        out_shape=jax.ShapeDtypeStruct((COLUMN, WIDE), F32),
        name="merge_plane",
    )(partial.reshape(CHIPS, WIDE))
    merged = lax.all_to_all(merged, ("z_lo", "z_hi"), 0, 0, tiled=True)
    vmem = pl.BlockSpec(memory_space=pltpu.VMEM)
    return pl.pallas_call(
        merge_column,
        in_specs=[pl.BlockSpec(memory_space=pltpu.SMEM), vmem, vmem],
        out_specs=vmem,
        out_shape=jax.ShapeDtypeStruct((1, HEADS * VD), BF16),
        name="merge_column",
    )(lambdas, merged, norm_gain.reshape(1, HEADS * VD))


def solution(mesh):
    fine = Mesh(mesh.devices.reshape(4, 2, 4, 4, 2), AXES)
    rows = P(AXES, None)
    return jax.shard_map(
        shards,
        mesh=fine,
        in_specs=(rows, rows, rows, P(), P()),
        out_specs=rows,
        check_vma=False,
    )
```

```python
import math

import jax
import jax.numpy as jnp
from jax import lax
from jax.experimental import pallas as pl
from jax.experimental.pallas import tpu as pltpu
from jax.sharding import Mesh, PartitionSpec as P

HEADS = 8
MAPS = 16
HD = 128
VD = 256
KEYS = 256
DEVICES = 256
CHIPS = 128
PLANE = 16
COLUMN = 8
SUMS = MAPS * VD
WIDE = SUMS + 128
LINES = 40
NEG = -1e30
AXES = ("x", "z_lo", "y", "z_hi", "core")
BF16 = jnp.bfloat16
F32 = jnp.float32


def attend(place_ref, q_ref, ka_ref, va_ref, kb_ref, vb_ref, out_ref):
    place = place_ref[0]
    core = place % 2
    row = lax.broadcasted_iota(jnp.int32, (CHIPS, 1), 0)
    device = (row // 32) * 64 + ((row // 4) % 2) * 32 + ((row // 8) % 4) * 8 + (row % 4) * 2 + core
    last = device + (DEVICES - 1) * KEYS
    last_a = last - place * KEYS
    last_b = last - (place + 1 - 2 * core) * KEYS
    key = lax.broadcasted_iota(jnp.int32, (CHIPS, KEYS), 1)
    lane = lax.broadcasted_iota(jnp.int32, (CHIPS, 128), 1)
    scaling = math.log2(math.e) / math.sqrt(HD)
    trans = (((1,), (1,)), ((), ()))
    stats = jnp.zeros((CHIPS, 128), F32)
    for index in range(MAPS):
        cols = slice(index * HD, (index + 1) * HD)
        v_cols = slice(index // 2 * VD, (index // 2 + 1) * VD)
        q = q_ref[:, cols]
        sa = lax.dot_general(q, ka_ref[:, cols], trans, preferred_element_type=F32) * scaling
        sb = lax.dot_general(q, kb_ref[:, cols], trans, preferred_element_type=F32) * scaling
        sa = jnp.where(key <= last_a, sa, NEG)
        sb = jnp.where(key <= last_b, sb, NEG)
        top = jnp.max(jnp.maximum(sa, sb), axis=1, keepdims=True).astype(BF16).astype(F32)
        ea = jnp.exp2(sa - top)
        eb = jnp.exp2(sb - top)
        total = jnp.sum(ea + eb, axis=1, keepdims=True)
        acc = jnp.dot(ea.astype(BF16), va_ref[:, v_cols], preferred_element_type=F32)
        acc += jnp.dot(eb.astype(BF16), vb_ref[:, v_cols], preferred_element_type=F32)
        out_ref[:, index * VD : (index + 1) * VD] = acc.astype(BF16)
        high = total.astype(BF16).astype(F32)
        stats = jnp.where(lane == index, top, stats)
        stats = jnp.where(lane == index + MAPS, high, stats)
        stats = jnp.where(lane == index + 2 * MAPS, total - high, stats)
    out_ref[:, SUMS:] = stats.astype(BF16)


def merge_plane(in_ref, out_ref):
    stats = in_ref[:, SUMS:].astype(F32)
    total = pltpu.roll(stats, 128 - MAPS, 1) + pltpu.roll(stats, 128 - 2 * MAPS, 1)
    stats = stats.reshape(PLANE, COLUMN, 128)
    total = total.reshape(PLANE, COLUMN, 128)
    top = jnp.max(stats, axis=0)
    weight = jnp.exp2(stats - top[None])
    total = jnp.sum(weight * total, axis=0)
    lane = lax.broadcasted_iota(jnp.int32, (COLUMN, 128), 1)
    out_ref[pl.ds(2 * MAPS, COLUMN, stride=LINES), :] = jnp.where(
        lane < MAPS, top, pltpu.roll(total, MAPS, 1)
    )
    for line in range(2 * MAPS):
        part = in_ref[:, line * 128 : (line + 1) * 128].astype(F32).reshape(PLANE, COLUMN, 128)
        index = line // 2
        out_ref[pl.ds(line, COLUMN, stride=LINES), :] = jnp.sum(
            part * weight[:, :, index : index + 1], axis=0
        )


def merge_column(lam_ref, in_ref, gain_ref, out_ref):
    stats = in_ref[pl.ds(2 * MAPS, COLUMN, stride=LINES), :]
    total = pltpu.roll(stats, 128 - MAPS, 1)
    top = jnp.max(stats, axis=0, keepdims=True)
    weight = jnp.exp2(stats - top)
    lane = lax.broadcasted_iota(jnp.int32, (COLUMN, 128), 1)
    total = jnp.where(lane < MAPS, jnp.sum(weight * total, axis=0, keepdims=True), 1.0)
    weight = weight / total
    for head in range(HEADS):
        one = weight[:, 2 * head : 2 * head + 1]
        two = weight[:, 2 * head + 1 : 2 * head + 2] * lam_ref[head]
        halves = []
        for half in range(2):
            first = in_ref[pl.ds(4 * head + half, COLUMN, stride=LINES), :] * one
            second = in_ref[pl.ds(4 * head + 2 + half, COLUMN, stride=LINES), :] * two
            halves.append(jnp.sum(first - second, axis=0, keepdims=True))
        diff = jnp.concatenate(halves, axis=1)
        meansq = jnp.mean(diff * diff, axis=1, keepdims=True)
        cols = slice(head * VD, (head + 1) * VD)
        out_ref[:, cols] = (diff / jnp.sqrt(meansq + 1e-5) * gain_ref[:, cols]).astype(BF16)


def shards(queries, key_maps, values, lambdas, norm_gain):
    swap = [(0, 1), (1, 0)]
    key_other = lax.ppermute(key_maps, "core", swap)
    value_other = lax.ppermute(values, "core", swap)
    place = lax.axis_index(AXES).astype(jnp.int32).reshape(1)

    spread = jnp.broadcast_to(queries.reshape(1, MAPS, HD), (COLUMN, MAPS, HD))
    column = lax.all_to_all(spread, ("z_lo", "z_hi"), 0, 0, tiled=True)
    column = column.reshape(1, COLUMN, MAPS * HD)
    spread = jnp.broadcast_to(column, (PLANE, COLUMN, MAPS * HD))
    q_all = lax.all_to_all(spread, ("x", "y"), 0, 0, tiled=True).reshape(CHIPS, MAPS * HD)

    smem = pl.BlockSpec(memory_space=pltpu.SMEM)
    vmem = pl.BlockSpec(memory_space=pltpu.VMEM)
    partial = pl.pallas_call(
        attend,
        in_specs=[smem, vmem, vmem, vmem, vmem, vmem],
        out_specs=vmem,
        out_shape=jax.ShapeDtypeStruct((CHIPS, WIDE), BF16),
        compiler_params=pltpu.CompilerParams(vmem_limit_bytes=16 << 20),
        name="attend",
    )(place, q_all, key_maps, values, key_other, value_other)

    partial = partial.reshape(PLANE, COLUMN, WIDE)
    partial = lax.all_to_all(partial, ("x", "y"), 0, 0, tiled=True)
    merged = pl.pallas_call(
        merge_plane,
        in_specs=[vmem],
        out_specs=vmem,
        out_shape=jax.ShapeDtypeStruct((COLUMN * LINES, 128), F32),
        compiler_params=pltpu.CompilerParams(vmem_limit_bytes=8 << 20),
        name="merge_plane",
    )(partial.reshape(CHIPS, WIDE))
    merged = merged.reshape(COLUMN, LINES, 128)
    merged = lax.all_to_all(merged, ("z_lo", "z_hi"), 0, 0, tiled=True)
    return pl.pallas_call(
        merge_column,
        in_specs=[smem, vmem, vmem],
        out_specs=vmem,
        out_shape=jax.ShapeDtypeStruct((1, HEADS * VD), BF16),
        compiler_params=pltpu.CompilerParams(vmem_limit_bytes=8 << 20),
        name="merge_column",
    )(lambdas, merged.reshape(COLUMN * LINES, 128), norm_gain.reshape(1, HEADS * VD))


def solution(mesh):
    fine = Mesh(mesh.devices.reshape(4, 2, 4, 4, 2), AXES)
    rows = P(AXES, None)
    return jax.shard_map(
        shards,
        mesh=fine,
        in_specs=(rows, rows, rows, P(), P()),
        out_specs=rows,
        check_vma=False,
    )
```

```python
import math

import jax
import jax.numpy as jnp
from jax import lax
from jax.experimental import pallas as pl
from jax.experimental.pallas import tpu as pltpu
from jax.sharding import Mesh, PartitionSpec as P

HEADS = 8
MAPS = 16
HD = 128
VD = 256
KEYS = 256
DEVICES = 256
CHIPS = 128
PLANE = 16
COLUMN = 8
SUMS = MAPS * VD
WIDE = SUMS + 128
LINES = 40
LAG = 4
NEG = -1e30
AXES = ("x", "z_lo", "y", "z_hi", "core")
BF16 = jnp.bfloat16
F32 = jnp.float32


def repeat_rows(in_ref, out_ref):
    rows = in_ref[...].astype(F32)
    rows = jnp.concatenate([rows, rows], axis=0).astype(BF16)
    for start in range(0, CHIPS, 2 * COLUMN):
        out_ref[start : start + 2 * COLUMN, :] = rows


def attend(q_ref, ka_ref, kb_ref, va_ref, vb_ref, out_ref):
    core = lax.axis_index("core")
    place = (
        lax.axis_index("x") * 64
        + lax.axis_index("z_lo") * 32
        + lax.axis_index("y") * 8
        + lax.axis_index("z_hi") * 2
        + core
    )
    row = lax.broadcasted_iota(jnp.int32, (CHIPS, 1), 0)
    device = (row // 32) * 64 + ((row // 4) % 2) * 32 + ((row // 8) % 4) * 8 + (row % 4) * 2 + core
    last = device + (DEVICES - 1) * KEYS
    last_a = last - place * KEYS
    last_b = last - (place + 1 - 2 * core) * KEYS
    key = lax.broadcasted_iota(jnp.int32, (CHIPS, KEYS), 1)
    lane = lax.broadcasted_iota(jnp.int32, (CHIPS, 128), 1)
    scaling = math.log2(math.e) / math.sqrt(HD)
    trans = (((1,), (1,)), ((), ()))
    stats = jnp.zeros((CHIPS, 128), F32)
    waiting = []
    for index in range(MAPS + LAG):
        if index < MAPS:
            cols = slice(index * HD, (index + 1) * HD)
            q = q_ref[:, cols]
            sa = lax.dot_general(q, ka_ref[:, cols], trans, preferred_element_type=F32) * scaling
            sb = lax.dot_general(q, kb_ref[:, cols], trans, preferred_element_type=F32) * scaling
            sa = jnp.where(key <= last_a, sa, NEG)
            sb = jnp.where(key <= last_b, sb, NEG)
            top = jnp.max(jnp.maximum(sa, sb), axis=1, keepdims=True).astype(BF16).astype(F32)
            ea = jnp.exp2(sa - top)
            eb = jnp.exp2(sb - top)
            total = jnp.sum(ea + eb, axis=1, keepdims=True)
            waiting.append((ea.astype(BF16), eb.astype(BF16)))
            high = total.astype(BF16).astype(F32)
            stats = jnp.where(lane == index, top, stats)
            stats = jnp.where(lane == index + MAPS, high, stats)
            stats = jnp.where(lane == index + 2 * MAPS, total - high, stats)
        if index >= LAG:
            done = index - LAG
            cols = slice(done // 2 * VD, (done // 2 + 1) * VD)
            ea, eb = waiting[done]
            acc = jnp.dot(ea, va_ref[:, cols], preferred_element_type=F32)
            acc += jnp.dot(eb, vb_ref[:, cols], preferred_element_type=F32)
            out_ref[:, done * VD : (done + 1) * VD] = acc.astype(BF16)
    out_ref[:, SUMS:] = stats.astype(BF16)


def merge_plane(in_ref, out_ref, lines_ref):
    stats = in_ref[:, SUMS:].astype(F32)
    total = pltpu.roll(stats, 128 - MAPS, 1) + pltpu.roll(stats, 128 - 2 * MAPS, 1)
    stats = stats.reshape(PLANE, COLUMN, 128)
    total = total.reshape(PLANE, COLUMN, 128)
    top = jnp.max(stats, axis=0)
    weight = jnp.exp2(stats - top[None])
    total = jnp.sum(weight * total, axis=0)
    lane = lax.broadcasted_iota(jnp.int32, (COLUMN, 128), 1)
    high = total.astype(BF16).astype(F32)
    low = jnp.where(lane < 3 * MAPS, pltpu.roll(total - high, 2 * MAPS, 1), 0.0)
    tail = jnp.where(lane < 2 * MAPS, pltpu.roll(high, MAPS, 1), low)
    lines_ref[pl.ds(2 * MAPS, COLUMN, stride=LINES), :] = jnp.where(lane < MAPS, top, tail)
    for line in range(2 * MAPS + 1, LINES):
        lines_ref[pl.ds(line, COLUMN, stride=LINES), :] = jnp.zeros((COLUMN, 128), F32)
    for line in range(2 * MAPS):
        part = in_ref[:, line * 128 : (line + 1) * 128].astype(F32).reshape(PLANE, COLUMN, 128)
        index = line // 2
        lines_ref[pl.ds(line, COLUMN, stride=LINES), :] = jnp.sum(
            part * weight[:, :, index : index + 1], axis=0
        )
    out_ref[...] = lines_ref[...].astype(BF16)


def merge_column(lam_ref, in_ref, gain_ref, out_ref, lines_ref):
    lines_ref[...] = in_ref[...].astype(F32)
    stats = lines_ref[pl.ds(2 * MAPS, COLUMN, stride=LINES), :]
    total = pltpu.roll(stats, 128 - MAPS, 1) + pltpu.roll(stats, 128 - 2 * MAPS, 1)
    top = jnp.max(stats, axis=0, keepdims=True)
    weight = jnp.exp2(stats - top)
    lane = lax.broadcasted_iota(jnp.int32, (COLUMN, 128), 1)
    total = jnp.where(lane < MAPS, jnp.sum(weight * total, axis=0, keepdims=True), 1.0)
    weight = weight / total
    for head in range(HEADS):
        one = weight[:, 2 * head : 2 * head + 1]
        two = weight[:, 2 * head + 1 : 2 * head + 2] * lam_ref[:, head : head + 1]
        halves = []
        for half in range(2):
            first = lines_ref[pl.ds(4 * head + half, COLUMN, stride=LINES), :] * one
            second = lines_ref[pl.ds(4 * head + 2 + half, COLUMN, stride=LINES), :] * two
            halves.append(jnp.sum(first - second, axis=0, keepdims=True))
        squares = halves[0] * halves[0] + halves[1] * halves[1]
        meansq = jnp.sum(squares, axis=1, keepdims=True) / VD
        factor = 1.0 / jnp.sqrt(meansq + 1e-5)
        for half in range(2):
            cols = slice(head * VD + half * 128, head * VD + half * 128 + 128)
            out_ref[:, cols] = (halves[half] * factor * gain_ref[:, cols]).astype(BF16)


def shards(queries, key_maps, values, lambdas, norm_gain):
    swap = [(0, 1), (1, 0)]
    key_other = lax.ppermute(key_maps, "core", swap)
    value_other = lax.ppermute(values, "core", swap)

    spread = jnp.broadcast_to(queries.reshape(1, MAPS, HD), (COLUMN, MAPS, HD))
    column = lax.all_to_all(spread, ("z_lo", "z_hi"), 0, 0, tiled=True)
    column = column.reshape(COLUMN, MAPS * HD)
    vmem = pl.BlockSpec(memory_space=pltpu.VMEM)
    spread = pl.pallas_call(
        repeat_rows,
        in_specs=[vmem],
        out_specs=vmem,
        out_shape=jax.ShapeDtypeStruct((CHIPS, MAPS * HD), BF16),
        compiler_params=pltpu.CompilerParams(vmem_limit_bytes=8 << 20),
        cost_estimate=pl.CostEstimate(flops=1 << 31, bytes_accessed=1 << 20, transcendentals=0),
        name="repeat_rows",
    )(column)
    spread = spread.reshape(PLANE, COLUMN, MAPS * HD)
    q_all = lax.all_to_all(spread, ("x", "y"), 0, 0, tiled=True).reshape(CHIPS, MAPS * HD)

    partial = pl.pallas_call(
        attend,
        in_specs=[vmem] * 5,
        out_specs=vmem,
        out_shape=jax.ShapeDtypeStruct((CHIPS, WIDE), BF16),
        compiler_params=pltpu.CompilerParams(vmem_limit_bytes=16 << 20),
        name="attend",
    )(q_all, key_maps, key_other, values, value_other)

    partial = partial.reshape(PLANE, COLUMN, WIDE)
    partial = lax.all_to_all(partial, ("x", "y"), 0, 0, tiled=True)
    merged = pl.pallas_call(
        merge_plane,
        in_specs=[vmem],
        out_specs=vmem,
        out_shape=jax.ShapeDtypeStruct((COLUMN * LINES, 128), BF16),
        scratch_shapes=[pltpu.VMEM((COLUMN * LINES, 128), F32)],
        compiler_params=pltpu.CompilerParams(vmem_limit_bytes=8 << 20),
        name="merge_plane",
    )(partial.reshape(CHIPS, WIDE))
    merged = merged.reshape(COLUMN, LINES, 128)
    merged = lax.all_to_all(merged, ("z_lo", "z_hi"), 0, 0, tiled=True)
    return pl.pallas_call(
        merge_column,
        in_specs=[vmem, vmem, vmem],
        out_specs=vmem,
        out_shape=jax.ShapeDtypeStruct((1, HEADS * VD), BF16),
        scratch_shapes=[pltpu.VMEM((COLUMN * LINES, 128), F32)],
        compiler_params=pltpu.CompilerParams(vmem_limit_bytes=8 << 20),
        name="merge_column",
    )(lambdas.reshape(1, HEADS), merged.reshape(COLUMN * LINES, 128), norm_gain.reshape(1, HEADS * VD))


def solution(mesh):
    fine = Mesh(mesh.devices.reshape(4, 2, 4, 4, 2), AXES)
    rows = P(AXES, None)
    return jax.shard_map(
        shards,
        mesh=fine,
        in_specs=(rows, rows, rows, P(), P()),
        out_specs=rows,
        check_vma=False,
    )
```

```python
import math

import jax
import jax.numpy as jnp
from jax import lax
from jax.experimental import pallas as pl
from jax.experimental.pallas import tpu as pltpu
from jax.sharding import Mesh, PartitionSpec as P

HEADS = 8
MAPS = 16
HD = 128
VD = 256
KEYS = 256
DEVICES = 256
CHIPS = 128
PLANE = 16
COLUMN = 8
SUMS = MAPS * VD
WIDE = SUMS + 128
LINES = 40
LAG = 3
NEG = -1e30
AXES = ("x", "z_lo", "y", "z_hi", "core")
BF16 = jnp.bfloat16
F32 = jnp.float32


def repeat_rows(in_ref, out_ref):
    rows = in_ref[...].astype(F32)
    rows = jnp.concatenate([rows, rows], axis=0).astype(BF16)
    for start in range(0, CHIPS, 2 * COLUMN):
        out_ref[start : start + 2 * COLUMN, :] = rows


def attend(q_ref, ka_ref, kb_ref, va_ref, vb_ref, out_ref, mask_ref):
    core = lax.axis_index("core")
    place = (
        lax.axis_index("x") * 64
        + lax.axis_index("z_lo") * 32
        + lax.axis_index("y") * 8
        + lax.axis_index("z_hi") * 2
        + core
    )
    row = lax.broadcasted_iota(jnp.int32, (CHIPS, 1), 0)
    device = (row // 32) * 64 + ((row // 4) % 2) * 32 + ((row // 8) % 4) * 8 + (row % 4) * 2 + core
    last = device + (DEVICES - 1) * KEYS
    last_a = last - place * KEYS
    last_b = last - (place + 1 - 2 * core) * KEYS
    key = lax.broadcasted_iota(jnp.int32, (CHIPS, KEYS), 1)
    mask_ref[:, :KEYS] = jnp.where(key <= last_a, 0.0, NEG)
    mask_ref[:, KEYS:] = jnp.where(key <= last_b, 0.0, NEG)
    lane = lax.broadcasted_iota(jnp.int32, (CHIPS, 128), 1)
    scaling = math.log2(math.e) / math.sqrt(HD)
    trans = (((1,), (1,)), ((), ()))
    stats = jnp.zeros((CHIPS, 128), F32)
    waiting = []
    for index in range(MAPS + LAG):
        if index < MAPS:
            cols = slice(index * HD, (index + 1) * HD)
            q = q_ref[:, cols]
            sa = lax.dot_general(q, ka_ref[:, cols], trans, preferred_element_type=F32) * scaling
            sb = lax.dot_general(q, kb_ref[:, cols], trans, preferred_element_type=F32) * scaling
            sa = sa + mask_ref[:, :KEYS]
            sb = sb + mask_ref[:, KEYS:]
            top = jnp.max(jnp.maximum(sa, sb), axis=1, keepdims=True).astype(BF16).astype(F32)
            ea = jnp.exp2(sa - top)
            eb = jnp.exp2(sb - top)
            total = jnp.sum(ea + eb, axis=1, keepdims=True)
            waiting.append((ea.astype(BF16), eb.astype(BF16)))
            stats = jnp.where(lane == index, top, stats)
            stats = jnp.where(lane == index + MAPS, total, stats)
        if index >= LAG:
            done = index - LAG
            cols = slice(done // 2 * VD, (done // 2 + 1) * VD)
            ea, eb = waiting[done]
            acc = jnp.dot(ea, va_ref[:, cols], preferred_element_type=F32)
            acc += jnp.dot(eb, vb_ref[:, cols], preferred_element_type=F32)
            out_ref[:, done * VD : (done + 1) * VD] = acc.astype(BF16)
    high = stats.astype(BF16).astype(F32)
    low = jnp.where(lane < 3 * MAPS, pltpu.roll(stats - high, MAPS, 1), 0.0)
    out_ref[:, SUMS:] = jnp.where(lane < 2 * MAPS, high, low).astype(BF16)


def merge_plane(in_ref, out_ref, lines_ref):
    stats = in_ref[:, SUMS:].astype(F32)
    total = pltpu.roll(stats, 128 - MAPS, 1) + pltpu.roll(stats, 128 - 2 * MAPS, 1)
    stats = stats.reshape(PLANE, COLUMN, 128)
    total = total.reshape(PLANE, COLUMN, 128)
    top = jnp.max(stats, axis=0)
    weight = jnp.exp2(stats - top[None])
    total = jnp.sum(weight * total, axis=0)
    lane = lax.broadcasted_iota(jnp.int32, (COLUMN, 128), 1)
    high = total.astype(BF16).astype(F32)
    low = jnp.where(lane < 3 * MAPS, pltpu.roll(total - high, 2 * MAPS, 1), 0.0)
    tail = jnp.where(lane < 2 * MAPS, pltpu.roll(high, MAPS, 1), low)
    lines_ref[pl.ds(2 * MAPS, COLUMN, stride=LINES), :] = jnp.where(lane < MAPS, top, tail)
    for line in range(2 * MAPS + 1, LINES):
        lines_ref[pl.ds(line, COLUMN, stride=LINES), :] = jnp.zeros((COLUMN, 128), F32)
    for line in range(2 * MAPS):
        part = in_ref[:, line * 128 : (line + 1) * 128].astype(F32).reshape(PLANE, COLUMN, 128)
        index = line // 2
        lines_ref[pl.ds(line, COLUMN, stride=LINES), :] = jnp.sum(
            part * weight[:, :, index : index + 1], axis=0
        )
    out_ref[...] = lines_ref[...].astype(BF16)


def merge_column(lam_ref, in_ref, gain_ref, out_ref, lines_ref):
    lines_ref[...] = in_ref[...].astype(F32)
    stats = lines_ref[pl.ds(2 * MAPS, COLUMN, stride=LINES), :]
    total = pltpu.roll(stats, 128 - MAPS, 1) + pltpu.roll(stats, 128 - 2 * MAPS, 1)
    top = jnp.max(stats, axis=0, keepdims=True)
    weight = jnp.exp2(stats - top)
    lane = lax.broadcasted_iota(jnp.int32, (COLUMN, 128), 1)
    total = jnp.where(lane < MAPS, jnp.sum(weight * total, axis=0, keepdims=True), 1.0)
    weight = weight / total
    for head in range(HEADS):
        one = weight[:, 2 * head : 2 * head + 1]
        two = weight[:, 2 * head + 1 : 2 * head + 2] * lam_ref[:, head : head + 1]
        halves = []
        for half in range(2):
            first = lines_ref[pl.ds(4 * head + half, COLUMN, stride=LINES), :] * one
            second = lines_ref[pl.ds(4 * head + 2 + half, COLUMN, stride=LINES), :] * two
            halves.append(jnp.sum(first - second, axis=0, keepdims=True))
        squares = halves[0] * halves[0] + halves[1] * halves[1]
        meansq = jnp.sum(squares, axis=1, keepdims=True) / VD
        factor = 1.0 / jnp.sqrt(meansq + 1e-5)
        for half in range(2):
            cols = slice(head * VD + half * 128, head * VD + half * 128 + 128)
            out_ref[:, cols] = (halves[half] * factor * gain_ref[:, cols]).astype(BF16)


def shards(queries, key_maps, values, lambdas, norm_gain):
    swap = [(0, 1), (1, 0)]
    key_other = lax.ppermute(key_maps, "core", swap)
    value_other = lax.ppermute(values, "core", swap)

    spread = jnp.broadcast_to(queries.reshape(1, MAPS, HD), (COLUMN, MAPS, HD))
    column = lax.all_to_all(spread, ("z_lo", "z_hi"), 0, 0, tiled=True)
    column = column.reshape(COLUMN, MAPS * HD)
    vmem = pl.BlockSpec(memory_space=pltpu.VMEM)
    spread = pl.pallas_call(
        repeat_rows,
        in_specs=[vmem],
        out_specs=vmem,
        out_shape=jax.ShapeDtypeStruct((CHIPS, MAPS * HD), BF16),
        compiler_params=pltpu.CompilerParams(vmem_limit_bytes=8 << 20),
        cost_estimate=pl.CostEstimate(flops=1 << 34, bytes_accessed=1 << 20, transcendentals=0),
        name="repeat_rows",
    )(column)
    spread = spread.reshape(PLANE, COLUMN, MAPS * HD)
    q_all = lax.all_to_all(spread, ("x", "y"), 0, 0, tiled=True).reshape(CHIPS, MAPS * HD)

    partial = pl.pallas_call(
        attend,
        in_specs=[vmem] * 5,
        out_specs=vmem,
        out_shape=jax.ShapeDtypeStruct((CHIPS, WIDE), BF16),
        scratch_shapes=[pltpu.VMEM((CHIPS, 2 * KEYS), F32)],
        compiler_params=pltpu.CompilerParams(vmem_limit_bytes=16 << 20),
        name="attend",
    )(q_all, key_maps, key_other, values, value_other)

    partial = partial.reshape(PLANE, COLUMN, WIDE)
    partial = lax.all_to_all(partial, ("x", "y"), 0, 0, tiled=True)
    merged = pl.pallas_call(
        merge_plane,
        in_specs=[vmem],
        out_specs=vmem,
        out_shape=jax.ShapeDtypeStruct((COLUMN * LINES, 128), BF16),
        scratch_shapes=[pltpu.VMEM((COLUMN * LINES, 128), F32)],
        compiler_params=pltpu.CompilerParams(vmem_limit_bytes=8 << 20),
        name="merge_plane",
    )(partial.reshape(CHIPS, WIDE))
    merged = merged.reshape(COLUMN, LINES, 128)
    merged = lax.all_to_all(merged, ("z_lo", "z_hi"), 0, 0, tiled=True)
    return pl.pallas_call(
        merge_column,
        in_specs=[vmem, vmem, vmem],
        out_specs=vmem,
        out_shape=jax.ShapeDtypeStruct((1, HEADS * VD), BF16),
        scratch_shapes=[pltpu.VMEM((COLUMN * LINES, 128), F32)],
        compiler_params=pltpu.CompilerParams(vmem_limit_bytes=8 << 20),
        name="merge_column",
    )(lambdas.reshape(1, HEADS), merged.reshape(COLUMN * LINES, 128), norm_gain.reshape(1, HEADS * VD))


def solution(mesh):
    fine = Mesh(mesh.devices.reshape(4, 2, 4, 4, 2), AXES)
    rows = P(AXES, None)
    return jax.shard_map(
        shards,
        mesh=fine,
        in_specs=(rows, rows, rows, P(), P()),
        out_specs=rows,
        check_vma=False,
    )
```

```python
import math

import jax
import jax.numpy as jnp
from jax import lax
from jax.experimental import pallas as pl
from jax.experimental.pallas import tpu as pltpu
from jax.sharding import Mesh, PartitionSpec as P

HEADS = 8
MAPS = 16
HD = 128
VD = 256
KEYS = 256
DEVICES = 256
CHIPS = 128
PLANE = 16
COLUMN = 8
SUMS = MAPS * VD
WIDE = SUMS + 128
LINES = 40
LAG = 3
NEG = -1e30
AXES = ("x", "z_lo", "y", "z_hi", "core")
BF16 = jnp.bfloat16
F32 = jnp.float32


def causal_mask(mask_ref):
    core = lax.axis_index("core")
    place = (
        lax.axis_index("x") * 64
        + lax.axis_index("z_lo") * 32
        + lax.axis_index("y") * 8
        + lax.axis_index("z_hi") * 2
        + core
    )
    row = lax.broadcasted_iota(jnp.int32, (CHIPS, 1), 0)
    device = (row // 32) * 64 + ((row // 4) % 2) * 32 + ((row // 8) % 4) * 8 + (row % 4) * 2 + core
    last = device + (DEVICES - 1) * KEYS
    last_a = last - place * KEYS
    last_b = last - (place + 1 - 2 * core) * KEYS
    key = lax.broadcasted_iota(jnp.int32, (CHIPS, KEYS), 1)
    mask_ref[:, :KEYS] = jnp.where(key <= last_a, 0.0, NEG)
    mask_ref[:, KEYS:] = jnp.where(key <= last_b, 0.0, NEG)


def own_row(in_ref, mask_ref, out_ref):
    row = in_ref[...].astype(F32)
    tall = jnp.concatenate([row[:, start * HD : (start + 1) * HD] for start in range(MAPS)], axis=0)
    tall = tall.astype(BF16)
    for copy in range(COLUMN):
        out_ref[copy] = tall


def repeat_rows(in_ref, out_ref):
    rows = in_ref[...].astype(F32)
    rows = jnp.concatenate([rows, rows], axis=0).astype(BF16)
    for start in range(0, CHIPS, 2 * COLUMN):
        out_ref[start : start + 2 * COLUMN, :] = rows


def attend(q_ref, ka_ref, kb_ref, va_ref, vb_ref, mask_ref, out_ref):
    lane = lax.broadcasted_iota(jnp.int32, (CHIPS, 128), 1)
    scaling = math.log2(math.e) / math.sqrt(HD)
    trans = (((1,), (1,)), ((), ()))
    stats = jnp.zeros((CHIPS, 128), F32)
    waiting = []
    for index in range(MAPS + LAG):
        if index < MAPS:
            cols = slice(index * HD, (index + 1) * HD)
            q = q_ref[:, cols]
            sa = lax.dot_general(q, ka_ref[:, cols], trans, preferred_element_type=F32) * scaling
            sb = lax.dot_general(q, kb_ref[:, cols], trans, preferred_element_type=F32) * scaling
            sa = sa + mask_ref[:, :KEYS]
            sb = sb + mask_ref[:, KEYS:]
            top = jnp.max(jnp.maximum(sa, sb), axis=1, keepdims=True).astype(BF16).astype(F32)
            ea = jnp.exp2(sa - top)
            eb = jnp.exp2(sb - top)
            total = jnp.sum(ea + eb, axis=1, keepdims=True)
            waiting.append((ea.astype(BF16), eb.astype(BF16)))
            stats = jnp.where(lane == index, top, stats)
            stats = jnp.where(lane == index + MAPS, total, stats)
        if index >= LAG:
            done = index - LAG
            cols = slice(done // 2 * VD, (done // 2 + 1) * VD)
            ea, eb = waiting[done]
            acc = jnp.dot(ea, va_ref[:, cols], preferred_element_type=F32)
            acc += jnp.dot(eb, vb_ref[:, cols], preferred_element_type=F32)
            out_ref[:, done * VD : (done + 1) * VD] = acc.astype(BF16)
    high = stats.astype(BF16).astype(F32)
    low = jnp.where(lane < 3 * MAPS, pltpu.roll(stats - high, MAPS, 1), 0.0)
    out_ref[:, SUMS:] = jnp.where(lane < 2 * MAPS, high, low).astype(BF16)


def merge_plane(in_ref, out_ref, lines_ref):
    stats = in_ref[:, SUMS:].astype(F32)
    total = pltpu.roll(stats, 128 - MAPS, 1) + pltpu.roll(stats, 128 - 2 * MAPS, 1)
    stats = stats.reshape(PLANE, COLUMN, 128)
    total = total.reshape(PLANE, COLUMN, 128)
    top = jnp.max(stats, axis=0)
    weight = jnp.exp2(stats - top[None])
    total = jnp.sum(weight * total, axis=0)
    lane = lax.broadcasted_iota(jnp.int32, (COLUMN, 128), 1)
    high = total.astype(BF16).astype(F32)
    low = jnp.where(lane < 3 * MAPS, pltpu.roll(total - high, 2 * MAPS, 1), 0.0)
    tail = jnp.where(lane < 2 * MAPS, pltpu.roll(high, MAPS, 1), low)
    lines_ref[pl.ds(2 * MAPS, COLUMN, stride=LINES), :] = jnp.where(lane < MAPS, top, tail)
    for line in range(2 * MAPS + 1, LINES):
        lines_ref[pl.ds(line, COLUMN, stride=LINES), :] = jnp.zeros((COLUMN, 128), F32)
    for line in range(2 * MAPS):
        part = in_ref[:, line * 128 : (line + 1) * 128].astype(F32).reshape(PLANE, COLUMN, 128)
        index = line // 2
        lines_ref[pl.ds(line, COLUMN, stride=LINES), :] = jnp.sum(
            part * weight[:, :, index : index + 1], axis=0
        )
    out_ref[...] = lines_ref[...].astype(BF16)


def merge_column(lam_ref, in_ref, gain_ref, out_ref, lines_ref):
    lines_ref[...] = in_ref[...].astype(F32)
    stats = lines_ref[pl.ds(2 * MAPS, COLUMN, stride=LINES), :]
    total = pltpu.roll(stats, 128 - MAPS, 1) + pltpu.roll(stats, 128 - 2 * MAPS, 1)
    top = jnp.max(stats, axis=0, keepdims=True)
    weight = jnp.exp2(stats - top)
    lane = lax.broadcasted_iota(jnp.int32, (COLUMN, 128), 1)
    total = jnp.where(lane < MAPS, jnp.sum(weight * total, axis=0, keepdims=True), 1.0)
    weight = weight / total
    for head in range(HEADS):
        one = weight[:, 2 * head : 2 * head + 1]
        two = weight[:, 2 * head + 1 : 2 * head + 2] * lam_ref[:, head : head + 1]
        halves = []
        for half in range(2):
            first = lines_ref[pl.ds(4 * head + half, COLUMN, stride=LINES), :] * one
            second = lines_ref[pl.ds(4 * head + 2 + half, COLUMN, stride=LINES), :] * two
            halves.append(jnp.sum(first - second, axis=0, keepdims=True))
        squares = halves[0] * halves[0] + halves[1] * halves[1]
        meansq = jnp.sum(squares, axis=1, keepdims=True) / VD
        factor = 1.0 / jnp.sqrt(meansq + 1e-5)
        for half in range(2):
            cols = slice(head * VD + half * 128, head * VD + half * 128 + 128)
            out_ref[:, cols] = (halves[half] * factor * gain_ref[:, cols]).astype(BF16)


def shards(queries, key_maps, values, lambdas, norm_gain):
    swap = [(0, 1), (1, 0)]
    key_other = lax.ppermute(key_maps, "core", swap)
    value_other = lax.ppermute(values, "core", swap)

    vmem = pl.BlockSpec(memory_space=pltpu.VMEM)
    mask = pl.pallas_call(
        causal_mask,
        out_specs=vmem,
        out_shape=jax.ShapeDtypeStruct((CHIPS, 2 * KEYS), F32),
        compiler_params=pltpu.CompilerParams(vmem_limit_bytes=8 << 20),
        cost_estimate=pl.CostEstimate(flops=1 << 31, bytes_accessed=1 << 18, transcendentals=0),
        name="causal_mask",
    )()
    spread = pl.pallas_call(
        own_row,
        in_specs=[vmem, vmem],
        out_specs=vmem,
        out_shape=jax.ShapeDtypeStruct((COLUMN, MAPS, HD), BF16),
        compiler_params=pltpu.CompilerParams(vmem_limit_bytes=8 << 20),
        name="own_row",
    )(queries, mask)
    column = lax.all_to_all(spread, ("z_lo", "z_hi"), 0, 0, tiled=True)
    column = column.reshape(COLUMN, MAPS * HD)
    spread = pl.pallas_call(
        repeat_rows,
        in_specs=[vmem],
        out_specs=vmem,
        out_shape=jax.ShapeDtypeStruct((CHIPS, MAPS * HD), BF16),
        compiler_params=pltpu.CompilerParams(vmem_limit_bytes=8 << 20),
        cost_estimate=pl.CostEstimate(flops=1 << 31, bytes_accessed=1 << 20, transcendentals=0),
        name="repeat_rows",
    )(column)
    spread = spread.reshape(PLANE, COLUMN, MAPS * HD)
    q_all = lax.all_to_all(spread, ("x", "y"), 0, 0, tiled=True).reshape(CHIPS, MAPS * HD)

    partial = pl.pallas_call(
        attend,
        in_specs=[vmem] * 6,
        out_specs=vmem,
        out_shape=jax.ShapeDtypeStruct((CHIPS, WIDE), BF16),
        compiler_params=pltpu.CompilerParams(vmem_limit_bytes=16 << 20),
        name="attend",
    )(q_all, key_maps, key_other, values, value_other, mask)

    partial = partial.reshape(PLANE, COLUMN, WIDE)
    partial = lax.all_to_all(partial, ("x", "y"), 0, 0, tiled=True)
    merged = pl.pallas_call(
        merge_plane,
        in_specs=[vmem],
        out_specs=vmem,
        out_shape=jax.ShapeDtypeStruct((COLUMN * LINES, 128), BF16),
        scratch_shapes=[pltpu.VMEM((COLUMN * LINES, 128), F32)],
        compiler_params=pltpu.CompilerParams(vmem_limit_bytes=8 << 20),
        name="merge_plane",
    )(partial.reshape(CHIPS, WIDE))
    merged = merged.reshape(COLUMN, LINES, 128)
    merged = lax.all_to_all(merged, ("z_lo", "z_hi"), 0, 0, tiled=True)
    return pl.pallas_call(
        merge_column,
        in_specs=[vmem, vmem, vmem],
        out_specs=vmem,
        out_shape=jax.ShapeDtypeStruct((1, HEADS * VD), BF16),
        scratch_shapes=[pltpu.VMEM((COLUMN * LINES, 128), F32)],
        compiler_params=pltpu.CompilerParams(vmem_limit_bytes=8 << 20),
        name="merge_column",
    )(lambdas.reshape(1, HEADS), merged.reshape(COLUMN * LINES, 128), norm_gain.reshape(1, HEADS * VD))


def solution(mesh):
    fine = Mesh(mesh.devices.reshape(4, 2, 4, 4, 2), AXES)
    rows = P(AXES, None)
    return jax.shard_map(
        shards,
        mesh=fine,
        in_specs=(rows, rows, rows, P(), P()),
        out_specs=rows,
        check_vma=False,
    )
```

```python
import math

import jax
import jax.numpy as jnp
from jax import lax
from jax.experimental import pallas as pl
from jax.experimental.pallas import tpu as pltpu
from jax.sharding import Mesh, PartitionSpec as P

HEADS = 8
MAPS = 16
HD = 128
VD = 256
KEYS = 256
DEVICES = 256
CHIPS = 128
PLANE = 16
COLUMN = 8
SUMS = MAPS * VD
WIDE = SUMS + 128
LINES = 40
LAG = 3
NEG = -1e30
AXES = ("x1", "x0", "z0", "y1", "y0", "z2", "z1", "core")
PLANE_AXES = ("x0", "y1", "x1", "y0")
COLUMN_AXES = ("z0", "z1", "z2")
BF16 = jnp.bfloat16
F32 = jnp.float32


def causal_mask(mask_ref):
    core = lax.axis_index("core")
    place = core
    row = lax.broadcasted_iota(jnp.int32, (CHIPS, 1), 0)
    device = row * 0 + core
    for bit, axis in enumerate(reversed(PLANE_AXES + COLUMN_AXES)):
        weight = 1 << (len(AXES) - 1 - AXES.index(axis))
        place += lax.axis_index(axis) * weight
        device += ((row >> bit) & 1) * weight
    last = device + (DEVICES - 1) * KEYS
    last_a = last - place * KEYS
    last_b = last - (place + 1 - 2 * core) * KEYS
    key = lax.broadcasted_iota(jnp.int32, (CHIPS, KEYS), 1)
    mask_ref[:, :KEYS] = jnp.where(key <= last_a, 0.0, NEG)
    mask_ref[:, KEYS:] = jnp.where(key <= last_b, 0.0, NEG)


def own_row(in_ref, mask_ref, out_ref):
    row = in_ref[...].astype(F32)
    tall = jnp.concatenate([row[:, start * HD : (start + 1) * HD] for start in range(MAPS)], axis=0)
    tall = tall.astype(BF16)
    for copy in range(COLUMN):
        out_ref[copy] = tall


def repeat_rows(in_ref, out_ref):
    rows = in_ref[...].astype(F32)
    rows = jnp.concatenate([rows, rows], axis=0).astype(BF16)
    for start in range(0, CHIPS, 2 * COLUMN):
        out_ref[start : start + 2 * COLUMN, :] = rows


def attend(q_ref, ka_ref, kb_ref, va_ref, vb_ref, mask_ref, out_ref):
    lane = lax.broadcasted_iota(jnp.int32, (CHIPS, 128), 1)
    scaling = math.log2(math.e) / math.sqrt(HD)
    trans = (((1,), (1,)), ((), ()))
    stats = jnp.zeros((CHIPS, 128), F32)
    waiting = []
    for index in range(MAPS + LAG):
        if index < MAPS:
            cols = slice(index * HD, (index + 1) * HD)
            q = q_ref[:, cols]
            sa = lax.dot_general(q, ka_ref[:, cols], trans, preferred_element_type=F32) * scaling
            sb = lax.dot_general(q, kb_ref[:, cols], trans, preferred_element_type=F32) * scaling
            sa = sa + mask_ref[:, :KEYS]
            sb = sb + mask_ref[:, KEYS:]
            top = jnp.max(jnp.maximum(sa, sb), axis=1, keepdims=True).astype(BF16).astype(F32)
            ea = jnp.exp2(sa - top)
            eb = jnp.exp2(sb - top)
            total = jnp.sum(ea + eb, axis=1, keepdims=True)
            waiting.append((ea.astype(BF16), eb.astype(BF16)))
            stats = jnp.where(lane == index, top, stats)
            stats = jnp.where(lane == index + MAPS, total, stats)
        if index >= LAG:
            done = index - LAG
            cols = slice(done // 2 * VD, (done // 2 + 1) * VD)
            ea, eb = waiting[done]
            acc = jnp.dot(ea, va_ref[:, cols], preferred_element_type=F32)
            acc += jnp.dot(eb, vb_ref[:, cols], preferred_element_type=F32)
            out_ref[:, done * VD : (done + 1) * VD] = acc.astype(BF16)
    high = stats.astype(BF16).astype(F32)
    low = jnp.where(lane < 3 * MAPS, pltpu.roll(stats - high, MAPS, 1), 0.0)
    out_ref[:, SUMS:] = jnp.where(lane < 2 * MAPS, high, low).astype(BF16)


def merge_plane(in_ref, out_ref, lines_ref):
    stats = in_ref[:, SUMS:].astype(F32)
    total = pltpu.roll(stats, 128 - MAPS, 1) + pltpu.roll(stats, 128 - 2 * MAPS, 1)
    stats = stats.reshape(PLANE, COLUMN, 128)
    total = total.reshape(PLANE, COLUMN, 128)
    top = jnp.max(stats, axis=0)
    weight = jnp.exp2(stats - top[None])
    total = jnp.sum(weight * total, axis=0)
    lane = lax.broadcasted_iota(jnp.int32, (COLUMN, 128), 1)
    high = total.astype(BF16).astype(F32)
    low = jnp.where(lane < 3 * MAPS, pltpu.roll(total - high, 2 * MAPS, 1), 0.0)
    tail = jnp.where(lane < 2 * MAPS, pltpu.roll(high, MAPS, 1), low)
    lines_ref[pl.ds(2 * MAPS, COLUMN, stride=LINES), :] = jnp.where(lane < MAPS, top, tail)
    for line in range(2 * MAPS + 1, LINES):
        lines_ref[pl.ds(line, COLUMN, stride=LINES), :] = jnp.zeros((COLUMN, 128), F32)
    for line in range(2 * MAPS):
        part = in_ref[:, line * 128 : (line + 1) * 128].astype(F32).reshape(PLANE, COLUMN, 128)
        index = line // 2
        lines_ref[pl.ds(line, COLUMN, stride=LINES), :] = jnp.sum(
            part * weight[:, :, index : index + 1], axis=0
        )
    out_ref[...] = lines_ref[...].astype(BF16)


def merge_column(lam_ref, in_ref, gain_ref, out_ref, lines_ref):
    lines_ref[...] = in_ref[...].astype(F32)
    stats = lines_ref[pl.ds(2 * MAPS, COLUMN, stride=LINES), :]
    total = pltpu.roll(stats, 128 - MAPS, 1) + pltpu.roll(stats, 128 - 2 * MAPS, 1)
    top = jnp.max(stats, axis=0, keepdims=True)
    weight = jnp.exp2(stats - top)
    lane = lax.broadcasted_iota(jnp.int32, (COLUMN, 128), 1)
    total = jnp.where(lane < MAPS, jnp.sum(weight * total, axis=0, keepdims=True), 1.0)
    weight = weight / total
    for head in range(HEADS):
        one = weight[:, 2 * head : 2 * head + 1]
        two = weight[:, 2 * head + 1 : 2 * head + 2] * lam_ref[:, head : head + 1]
        halves = []
        for half in range(2):
            first = lines_ref[pl.ds(4 * head + half, COLUMN, stride=LINES), :] * one
            second = lines_ref[pl.ds(4 * head + 2 + half, COLUMN, stride=LINES), :] * two
            halves.append(jnp.sum(first - second, axis=0, keepdims=True))
        squares = halves[0] * halves[0] + halves[1] * halves[1]
        meansq = jnp.sum(squares, axis=1, keepdims=True) / VD
        factor = 1.0 / jnp.sqrt(meansq + 1e-5)
        for half in range(2):
            cols = slice(head * VD + half * 128, head * VD + half * 128 + 128)
            out_ref[:, cols] = (halves[half] * factor * gain_ref[:, cols]).astype(BF16)


def shards(queries, key_maps, values, lambdas, norm_gain):
    swap = [(0, 1), (1, 0)]
    key_other = lax.ppermute(key_maps, "core", swap)
    value_other = lax.ppermute(values, "core", swap)

    vmem = pl.BlockSpec(memory_space=pltpu.VMEM)
    mask = pl.pallas_call(
        causal_mask,
        out_specs=vmem,
        out_shape=jax.ShapeDtypeStruct((CHIPS, 2 * KEYS), F32),
        compiler_params=pltpu.CompilerParams(vmem_limit_bytes=8 << 20),
        cost_estimate=pl.CostEstimate(flops=1 << 31, bytes_accessed=1 << 18, transcendentals=0),
        name="causal_mask",
    )()
    spread = pl.pallas_call(
        own_row,
        in_specs=[vmem, vmem],
        out_specs=vmem,
        out_shape=jax.ShapeDtypeStruct((COLUMN, MAPS, HD), BF16),
        compiler_params=pltpu.CompilerParams(vmem_limit_bytes=8 << 20),
        name="own_row",
    )(queries, mask)
    column = lax.all_to_all(spread, COLUMN_AXES, 0, 0, tiled=True)
    column = column.reshape(COLUMN, MAPS * HD)
    spread = pl.pallas_call(
        repeat_rows,
        in_specs=[vmem],
        out_specs=vmem,
        out_shape=jax.ShapeDtypeStruct((CHIPS, MAPS * HD), BF16),
        compiler_params=pltpu.CompilerParams(vmem_limit_bytes=8 << 20),
        cost_estimate=pl.CostEstimate(flops=1 << 31, bytes_accessed=1 << 20, transcendentals=0),
        name="repeat_rows",
    )(column)
    spread = spread.reshape(PLANE, COLUMN, MAPS * HD)
    q_all = lax.all_to_all(spread, PLANE_AXES, 0, 0, tiled=True).reshape(CHIPS, MAPS * HD)

    partial = pl.pallas_call(
        attend,
        in_specs=[vmem] * 6,
        out_specs=vmem,
        out_shape=jax.ShapeDtypeStruct((CHIPS, WIDE), BF16),
        compiler_params=pltpu.CompilerParams(vmem_limit_bytes=16 << 20),
        name="attend",
    )(q_all, key_maps, key_other, values, value_other, mask)

    partial = partial.reshape(PLANE, COLUMN, WIDE)
    partial = lax.all_to_all(partial, PLANE_AXES, 0, 0, tiled=True)
    merged = pl.pallas_call(
        merge_plane,
        in_specs=[vmem],
        out_specs=vmem,
        out_shape=jax.ShapeDtypeStruct((COLUMN * LINES, 128), BF16),
        scratch_shapes=[pltpu.VMEM((COLUMN * LINES, 128), F32)],
        compiler_params=pltpu.CompilerParams(vmem_limit_bytes=8 << 20),
        name="merge_plane",
    )(partial.reshape(CHIPS, WIDE))
    merged = merged.reshape(COLUMN, LINES, 128)
    merged = lax.all_to_all(merged, COLUMN_AXES, 0, 0, tiled=True)
    return pl.pallas_call(
        merge_column,
        in_specs=[vmem, vmem, vmem],
        out_specs=vmem,
        out_shape=jax.ShapeDtypeStruct((1, HEADS * VD), BF16),
        scratch_shapes=[pltpu.VMEM((COLUMN * LINES, 128), F32)],
        compiler_params=pltpu.CompilerParams(vmem_limit_bytes=8 << 20),
        name="merge_column",
    )(lambdas.reshape(1, HEADS), merged.reshape(COLUMN * LINES, 128), norm_gain.reshape(1, HEADS * VD))


def solution(mesh):
    fine = Mesh(mesh.devices.reshape((2,) * len(AXES)), AXES)
    rows = P(AXES, None)
    return jax.shard_map(
        shards,
        mesh=fine,
        in_specs=(rows, rows, rows, P(), P()),
        out_specs=rows,
        check_vma=False,
    )
```

```python
import math

import jax
import jax.numpy as jnp
from jax import lax
from jax.experimental import pallas as pl
from jax.experimental.pallas import tpu as pltpu
from jax.sharding import Mesh, PartitionSpec as P

HEADS = 8
MAPS = 16
HD = 128
VD = 256
KEYS = 256
DEVICES = 256
CHIPS = 128
PLANE = 16
COLUMN = 8
SUMS = MAPS * VD
WIDE = SUMS + 128
LINES = 40
LAG = 3
NEG = -1e30
AXES = ("x1", "x0", "z0", "y1", "y0", "z2", "z1", "core")
PLANE_AXES = ("x0", "x1", "y1", "y0")
COLUMN_AXES = ("z0", "z1", "z2")
BF16 = jnp.bfloat16
F32 = jnp.float32


def causal_mask(mask_ref):
    core = lax.axis_index("core")
    place = core
    row = lax.broadcasted_iota(jnp.int32, (CHIPS, 1), 0)
    device = row * 0 + core
    for bit, axis in enumerate(reversed(PLANE_AXES + COLUMN_AXES)):
        weight = 1 << (len(AXES) - 1 - AXES.index(axis))
        place += lax.axis_index(axis) * weight
        device += ((row >> bit) & 1) * weight
    last = device + (DEVICES - 1) * KEYS
    last_a = last - place * KEYS
    last_b = last - (place + 1 - 2 * core) * KEYS
    key = lax.broadcasted_iota(jnp.int32, (CHIPS, KEYS), 1)
    mask_ref[:, :KEYS] = jnp.where(key <= last_a, 0.0, NEG)
    mask_ref[:, KEYS:] = jnp.where(key <= last_b, 0.0, NEG)


def own_row(in_ref, mask_ref, out_ref):
    row = in_ref[...].astype(F32)
    tall = jnp.concatenate([row[:, start * HD : (start + 1) * HD] for start in range(MAPS)], axis=0)
    tall = tall.astype(BF16)
    for copy in range(COLUMN):
        out_ref[copy] = tall


def repeat_rows(in_ref, out_ref):
    rows = in_ref[...].astype(F32)
    wide = jnp.concatenate([rows[:, index, :] for index in range(MAPS)], axis=1)
    wide = jnp.concatenate([wide, wide], axis=0).astype(BF16)
    for start in range(0, CHIPS, 2 * COLUMN):
        out_ref[start : start + 2 * COLUMN, :] = wide


def attend(q_ref, ka_ref, kb_ref, va_ref, vb_ref, mask_ref, out_ref):
    lane = lax.broadcasted_iota(jnp.int32, (CHIPS, 128), 1)
    scaling = math.log2(math.e) / math.sqrt(HD)
    trans = (((1,), (1,)), ((), ()))
    stats = jnp.zeros((CHIPS, 128), F32)
    waiting = []
    for index in range(MAPS + LAG):
        if index < MAPS:
            cols = slice(index * HD, (index + 1) * HD)
            q = q_ref[:, cols]
            sa = lax.dot_general(q, ka_ref[:, cols], trans, preferred_element_type=F32) * scaling
            sb = lax.dot_general(q, kb_ref[:, cols], trans, preferred_element_type=F32) * scaling
            sa = sa + mask_ref[:, :KEYS]
            sb = sb + mask_ref[:, KEYS:]
            top = jnp.max(jnp.maximum(sa, sb), axis=1, keepdims=True).astype(BF16).astype(F32)
            ea = jnp.exp2(sa - top)
            eb = jnp.exp2(sb - top)
            total = jnp.sum(ea + eb, axis=1, keepdims=True)
            waiting.append((ea.astype(BF16), eb.astype(BF16)))
            stats = jnp.where(lane == index, top, stats)
            stats = jnp.where(lane == index + MAPS, total, stats)
        if index >= LAG:
            done = index - LAG
            cols = slice(done // 2 * VD, (done // 2 + 1) * VD)
            ea, eb = waiting[done]
            acc = jnp.dot(ea, va_ref[:, cols], preferred_element_type=F32)
            acc += jnp.dot(eb, vb_ref[:, cols], preferred_element_type=F32)
            out_ref[:, done * VD : (done + 1) * VD] = acc.astype(BF16)
    high = stats.astype(BF16).astype(F32)
    low = jnp.where(lane < 3 * MAPS, pltpu.roll(stats - high, MAPS, 1), 0.0)
    out_ref[:, SUMS:] = jnp.where(lane < 2 * MAPS, high, low).astype(BF16)


def merge_plane(in_ref, out_ref, lines_ref):
    stats = in_ref[:, SUMS:].astype(F32)
    total = pltpu.roll(stats, 128 - MAPS, 1) + pltpu.roll(stats, 128 - 2 * MAPS, 1)
    stats = stats.reshape(PLANE, COLUMN, 128)
    total = total.reshape(PLANE, COLUMN, 128)
    top = jnp.max(stats, axis=0)
    weight = jnp.exp2(stats - top[None])
    total = jnp.sum(weight * total, axis=0)
    lane = lax.broadcasted_iota(jnp.int32, (COLUMN, 128), 1)
    high = total.astype(BF16).astype(F32)
    low = jnp.where(lane < 3 * MAPS, pltpu.roll(total - high, 2 * MAPS, 1), 0.0)
    tail = jnp.where(lane < 2 * MAPS, pltpu.roll(high, MAPS, 1), low)
    lines_ref[pl.ds(2 * MAPS, COLUMN, stride=LINES), :] = jnp.where(lane < MAPS, top, tail)
    for line in range(2 * MAPS + 1, LINES):
        lines_ref[pl.ds(line, COLUMN, stride=LINES), :] = jnp.zeros((COLUMN, 128), F32)
    for line in range(2 * MAPS):
        part = in_ref[:, line * 128 : (line + 1) * 128].astype(F32).reshape(PLANE, COLUMN, 128)
        index = line // 2
        lines_ref[pl.ds(line, COLUMN, stride=LINES), :] = jnp.sum(
            part * weight[:, :, index : index + 1], axis=0
        )
    out_ref[...] = lines_ref[...].astype(BF16)


def merge_column(lam_ref, in_ref, gain_ref, out_ref, lines_ref):
    lines_ref[...] = in_ref[...].astype(F32)
    stats = lines_ref[pl.ds(2 * MAPS, COLUMN, stride=LINES), :]
    total = pltpu.roll(stats, 128 - MAPS, 1) + pltpu.roll(stats, 128 - 2 * MAPS, 1)
    top = jnp.max(stats, axis=0, keepdims=True)
    weight = jnp.exp2(stats - top)
    lane = lax.broadcasted_iota(jnp.int32, (COLUMN, 128), 1)
    total = jnp.where(lane < MAPS, jnp.sum(weight * total, axis=0, keepdims=True), 1.0)
    weight = weight / total
    for head in range(HEADS):
        one = weight[:, 2 * head : 2 * head + 1]
        two = weight[:, 2 * head + 1 : 2 * head + 2] * lam_ref[:, head : head + 1]
        halves = []
        for half in range(2):
            first = lines_ref[pl.ds(4 * head + half, COLUMN, stride=LINES), :] * one
            second = lines_ref[pl.ds(4 * head + 2 + half, COLUMN, stride=LINES), :] * two
            halves.append(jnp.sum(first - second, axis=0, keepdims=True))
        squares = halves[0] * halves[0] + halves[1] * halves[1]
        meansq = jnp.sum(squares, axis=1, keepdims=True) / VD
        factor = 1.0 / jnp.sqrt(meansq + 1e-5)
        for half in range(2):
            cols = slice(head * VD + half * 128, head * VD + half * 128 + 128)
            out_ref[:, cols] = (halves[half] * factor * gain_ref[:, cols]).astype(BF16)


def shards(queries, key_maps, values, lambdas, norm_gain):
    swap = [(0, 1), (1, 0)]
    key_other = lax.ppermute(key_maps, "core", swap)
    value_other = lax.ppermute(values, "core", swap)

    vmem = pl.BlockSpec(memory_space=pltpu.VMEM)
    mask = pl.pallas_call(
        causal_mask,
        out_specs=vmem,
        out_shape=jax.ShapeDtypeStruct((CHIPS, 2 * KEYS), F32),
        compiler_params=pltpu.CompilerParams(vmem_limit_bytes=8 << 20),
        cost_estimate=pl.CostEstimate(flops=1 << 31, bytes_accessed=1 << 18, transcendentals=0),
        name="causal_mask",
    )()
    spread = pl.pallas_call(
        own_row,
        in_specs=[vmem, vmem],
        out_specs=vmem,
        out_shape=jax.ShapeDtypeStruct((COLUMN, MAPS, HD), BF16),
        compiler_params=pltpu.CompilerParams(vmem_limit_bytes=8 << 20),
        name="own_row",
    )(queries, mask)
    column = lax.all_to_all(spread, COLUMN_AXES, 0, 0, tiled=True)
    spread = pl.pallas_call(
        repeat_rows,
        in_specs=[vmem],
        out_specs=vmem,
        out_shape=jax.ShapeDtypeStruct((CHIPS, MAPS * HD), BF16),
        compiler_params=pltpu.CompilerParams(vmem_limit_bytes=8 << 20),
        cost_estimate=pl.CostEstimate(flops=1 << 31, bytes_accessed=1 << 20, transcendentals=0),
        name="repeat_rows",
    )(column)
    spread = spread.reshape(PLANE, COLUMN, MAPS * HD)
    q_all = lax.all_to_all(spread, PLANE_AXES, 0, 0, tiled=True).reshape(CHIPS, MAPS * HD)

    partial = pl.pallas_call(
        attend,
        in_specs=[vmem] * 6,
        out_specs=vmem,
        out_shape=jax.ShapeDtypeStruct((CHIPS, WIDE), BF16),
        compiler_params=pltpu.CompilerParams(vmem_limit_bytes=16 << 20),
        name="attend",
    )(q_all, key_maps, key_other, values, value_other, mask)

    partial = partial.reshape(PLANE, COLUMN, WIDE)
    partial = lax.all_to_all(partial, PLANE_AXES, 0, 0, tiled=True)
    merged = pl.pallas_call(
        merge_plane,
        in_specs=[vmem],
        out_specs=vmem,
        out_shape=jax.ShapeDtypeStruct((COLUMN * LINES, 128), BF16),
        scratch_shapes=[pltpu.VMEM((COLUMN * LINES, 128), F32)],
        compiler_params=pltpu.CompilerParams(vmem_limit_bytes=8 << 20),
        name="merge_plane",
    )(partial.reshape(CHIPS, WIDE))
    merged = merged.reshape(COLUMN, LINES, 128)
    merged = lax.all_to_all(merged, COLUMN_AXES, 0, 0, tiled=True)
    return pl.pallas_call(
        merge_column,
        in_specs=[vmem, vmem, vmem],
        out_specs=vmem,
        out_shape=jax.ShapeDtypeStruct((1, HEADS * VD), BF16),
        scratch_shapes=[pltpu.VMEM((COLUMN * LINES, 128), F32)],
        compiler_params=pltpu.CompilerParams(vmem_limit_bytes=8 << 20),
        name="merge_column",
    )(lambdas.reshape(1, HEADS), merged.reshape(COLUMN * LINES, 128), norm_gain.reshape(1, HEADS * VD))


def solution(mesh):
    fine = Mesh(mesh.devices.reshape((2,) * len(AXES)), AXES)
    rows = P(AXES, None)
    return jax.shard_map(
        shards,
        mesh=fine,
        in_specs=(rows, rows, rows, P(), P()),
        out_specs=rows,
        check_vma=False,
    )
```

```python
import math

import jax
import jax.numpy as jnp
from jax import lax
from jax.experimental import pallas as pl
from jax.experimental.pallas import tpu as pltpu
from jax.sharding import Mesh, PartitionSpec as P

HEADS = 8
MAPS = 16
HD = 128
VD = 256
KEYS = 256
DEVICES = 256
CHIPS = 128
PLANE = 16
COLUMN = 8
SUMS = MAPS * VD
WIDE = SUMS + 128
LINES = 40
LAG = 3
NEG = -1e30
AXES = ("x1", "x0", "z0", "y1", "y0", "z2", "z1", "core")
PLANE_AXES = ("x0", "x1", "y1", "y0")
COLUMN_AXES = ("z0", "z1", "z2")
BF16 = jnp.bfloat16
F32 = jnp.float32


def causal_mask(mask_ref):
    core = lax.axis_index("core")
    place = core
    row = lax.broadcasted_iota(jnp.int32, (CHIPS, 1), 0)
    device = row * 0 + core
    for bit, axis in enumerate(reversed(PLANE_AXES + COLUMN_AXES)):
        weight = 1 << (len(AXES) - 1 - AXES.index(axis))
        place += lax.axis_index(axis) * weight
        device += ((row >> bit) & 1) * weight
    last = device + (DEVICES - 1) * KEYS
    last_a = last - place * KEYS
    last_b = last - (place + 1 - 2 * core) * KEYS
    key = lax.broadcasted_iota(jnp.int32, (CHIPS, KEYS), 1)
    mask_ref[:, :KEYS] = jnp.where(key <= last_a, 0.0, NEG)
    mask_ref[:, KEYS:] = jnp.where(key <= last_b, 0.0, NEG)


def own_row(in_ref, mask_ref, out_ref):
    row = in_ref[...].astype(F32)
    tall = jnp.concatenate([row[:, start * HD : (start + 1) * HD] for start in range(MAPS)], axis=0)
    tall = tall.astype(BF16)
    for copy in range(COLUMN):
        out_ref[copy] = tall


def repeat_rows(in_ref, out_ref):
    rows = in_ref[...].astype(F32)
    wide = jnp.concatenate([rows[:, index, :] for index in range(MAPS)], axis=1)
    wide = jnp.concatenate([wide, wide], axis=0).astype(BF16)
    for start in range(0, CHIPS, 2 * COLUMN):
        out_ref[start : start + 2 * COLUMN, :] = wide


def attend(q_ref, ka_ref, kb_ref, va_ref, vb_ref, mask_ref, out_ref):
    lane = lax.broadcasted_iota(jnp.int32, (CHIPS, 128), 1)
    scaling = math.log2(math.e) / math.sqrt(HD)
    trans = (((1,), (1,)), ((), ()))
    stats = jnp.zeros((CHIPS, 128), F32)
    waiting = []
    for index in range(MAPS + LAG):
        if index < MAPS:
            cols = slice(index * HD, (index + 1) * HD)
            q = q_ref[:, cols]
            sa = lax.dot_general(q, ka_ref[:, cols], trans, preferred_element_type=F32) * scaling
            sb = lax.dot_general(q, kb_ref[:, cols], trans, preferred_element_type=F32) * scaling
            sa = sa + mask_ref[:, :KEYS]
            sb = sb + mask_ref[:, KEYS:]
            wide = jnp.maximum(sa, sb)
            wide = jnp.maximum(wide[:, :HD], wide[:, HD:]).astype(BF16)
            top = jnp.max(wide, axis=1, keepdims=True).astype(F32)
            ea = jnp.exp2(sa - top)
            eb = jnp.exp2(sb - top)
            total = jnp.sum(ea + eb, axis=1, keepdims=True)
            waiting.append((ea.astype(BF16), eb.astype(BF16)))
            stats = jnp.where(lane == index, top, stats)
            stats = jnp.where(lane == index + MAPS, total, stats)
        if index >= LAG:
            done = index - LAG
            cols = slice(done // 2 * VD, (done // 2 + 1) * VD)
            ea, eb = waiting[done]
            acc = jnp.dot(ea, va_ref[:, cols], preferred_element_type=F32)
            acc += jnp.dot(eb, vb_ref[:, cols], preferred_element_type=F32)
            out_ref[:, done * VD : (done + 1) * VD] = acc.astype(BF16)
    high = stats.astype(BF16).astype(F32)
    low = jnp.where(lane < 3 * MAPS, pltpu.roll(stats - high, MAPS, 1), 0.0)
    out_ref[:, SUMS:] = jnp.where(lane < 2 * MAPS, high, low).astype(BF16)


def merge_plane(in_ref, out_ref, lines_ref):
    stats = in_ref[:, SUMS:].astype(F32)
    total = pltpu.roll(stats, 128 - MAPS, 1) + pltpu.roll(stats, 128 - 2 * MAPS, 1)
    stats = stats.reshape(PLANE, COLUMN, 128)
    total = total.reshape(PLANE, COLUMN, 128)
    top = jnp.max(stats, axis=0)
    weight = jnp.exp2(stats - top[None])
    total = jnp.sum(weight * total, axis=0)
    lane = lax.broadcasted_iota(jnp.int32, (COLUMN, 128), 1)
    high = total.astype(BF16).astype(F32)
    low = jnp.where(lane < 3 * MAPS, pltpu.roll(total - high, 2 * MAPS, 1), 0.0)
    tail = jnp.where(lane < 2 * MAPS, pltpu.roll(high, MAPS, 1), low)
    lines_ref[pl.ds(2 * MAPS, COLUMN, stride=LINES), :] = jnp.where(lane < MAPS, top, tail)
    for line in range(2 * MAPS + 1, LINES):
        lines_ref[pl.ds(line, COLUMN, stride=LINES), :] = jnp.zeros((COLUMN, 128), F32)
    for line in range(2 * MAPS):
        part = in_ref[:, line * 128 : (line + 1) * 128].astype(F32).reshape(PLANE, COLUMN, 128)
        index = line // 2
        lines_ref[pl.ds(line, COLUMN, stride=LINES), :] = jnp.sum(
            part * weight[:, :, index : index + 1], axis=0
        )
    out_ref[...] = lines_ref[...].astype(BF16)


def merge_column(lam_ref, in_ref, gain_ref, out_ref, lines_ref):
    lines_ref[...] = in_ref[...].astype(F32)
    stats = lines_ref[pl.ds(2 * MAPS, COLUMN, stride=LINES), :]
    total = pltpu.roll(stats, 128 - MAPS, 1) + pltpu.roll(stats, 128 - 2 * MAPS, 1)
    top = jnp.max(stats, axis=0, keepdims=True)
    weight = jnp.exp2(stats - top)
    lane = lax.broadcasted_iota(jnp.int32, (COLUMN, 128), 1)
    total = jnp.where(lane < MAPS, jnp.sum(weight * total, axis=0, keepdims=True), 1.0)
    weight = weight / total
    for head in range(HEADS):
        one = weight[:, 2 * head : 2 * head + 1]
        two = weight[:, 2 * head + 1 : 2 * head + 2] * lam_ref[:, head : head + 1]
        halves = []
        for half in range(2):
            first = lines_ref[pl.ds(4 * head + half, COLUMN, stride=LINES), :] * one
            second = lines_ref[pl.ds(4 * head + 2 + half, COLUMN, stride=LINES), :] * two
            halves.append(jnp.sum(first - second, axis=0, keepdims=True))
        squares = halves[0] * halves[0] + halves[1] * halves[1]
        meansq = jnp.sum(squares, axis=1, keepdims=True) / VD
        factor = 1.0 / jnp.sqrt(meansq + 1e-5)
        for half in range(2):
            cols = slice(head * VD + half * 128, head * VD + half * 128 + 128)
            out_ref[:, cols] = (halves[half] * factor * gain_ref[:, cols]).astype(BF16)


def shards(queries, key_maps, values, lambdas, norm_gain):
    swap = [(0, 1), (1, 0)]
    key_other = lax.ppermute(key_maps, "core", swap)
    value_other = lax.ppermute(values, "core", swap)

    vmem = pl.BlockSpec(memory_space=pltpu.VMEM)
    mask = pl.pallas_call(
        causal_mask,
        out_specs=vmem,
        out_shape=jax.ShapeDtypeStruct((CHIPS, 2 * KEYS), F32),
        compiler_params=pltpu.CompilerParams(vmem_limit_bytes=8 << 20),
        cost_estimate=pl.CostEstimate(flops=1 << 31, bytes_accessed=1 << 18, transcendentals=0),
        name="causal_mask",
    )()
    spread = pl.pallas_call(
        own_row,
        in_specs=[vmem, vmem],
        out_specs=vmem,
        out_shape=jax.ShapeDtypeStruct((COLUMN, MAPS, HD), BF16),
        compiler_params=pltpu.CompilerParams(vmem_limit_bytes=8 << 20),
        name="own_row",
    )(queries, mask)
    column = lax.all_to_all(spread, COLUMN_AXES, 0, 0, tiled=True)
    spread = pl.pallas_call(
        repeat_rows,
        in_specs=[vmem],
        out_specs=vmem,
        out_shape=jax.ShapeDtypeStruct((CHIPS, MAPS * HD), BF16),
        compiler_params=pltpu.CompilerParams(vmem_limit_bytes=8 << 20),
        cost_estimate=pl.CostEstimate(flops=1 << 31, bytes_accessed=1 << 20, transcendentals=0),
        name="repeat_rows",
    )(column)
    spread = spread.reshape(PLANE, COLUMN, MAPS * HD)
    q_all = lax.all_to_all(spread, PLANE_AXES, 0, 0, tiled=True).reshape(CHIPS, MAPS * HD)

    partial = pl.pallas_call(
        attend,
        in_specs=[vmem] * 6,
        out_specs=vmem,
        out_shape=jax.ShapeDtypeStruct((CHIPS, WIDE), BF16),
        compiler_params=pltpu.CompilerParams(vmem_limit_bytes=16 << 20),
        name="attend",
    )(q_all, key_maps, key_other, values, value_other, mask)

    partial = partial.reshape(PLANE, COLUMN, WIDE)
    partial = lax.all_to_all(partial, PLANE_AXES, 0, 0, tiled=True)
    merged = pl.pallas_call(
        merge_plane,
        in_specs=[vmem],
        out_specs=vmem,
        out_shape=jax.ShapeDtypeStruct((COLUMN * LINES, 128), BF16),
        scratch_shapes=[pltpu.VMEM((COLUMN * LINES, 128), F32)],
        compiler_params=pltpu.CompilerParams(vmem_limit_bytes=8 << 20),
        name="merge_plane",
    )(partial.reshape(CHIPS, WIDE))
    merged = merged.reshape(COLUMN, LINES, 128)
    merged = lax.all_to_all(merged, COLUMN_AXES, 0, 0, tiled=True)
    return pl.pallas_call(
        merge_column,
        in_specs=[vmem, vmem, vmem],
        out_specs=vmem,
        out_shape=jax.ShapeDtypeStruct((1, HEADS * VD), BF16),
        scratch_shapes=[pltpu.VMEM((COLUMN * LINES, 128), F32)],
        compiler_params=pltpu.CompilerParams(vmem_limit_bytes=8 << 20),
        name="merge_column",
    )(lambdas.reshape(1, HEADS), merged.reshape(COLUMN * LINES, 128), norm_gain.reshape(1, HEADS * VD))


def solution(mesh):
    fine = Mesh(mesh.devices.reshape((2,) * len(AXES)), AXES)
    rows = P(AXES, None)
    return jax.shard_map(
        shards,
        mesh=fine,
        in_specs=(rows, rows, rows, P(), P()),
        out_specs=rows,
        check_vma=False,
    )
```

```python
import math

import jax
import jax.numpy as jnp
from jax import lax
from jax.experimental import pallas as pl
from jax.experimental.pallas import tpu as pltpu
from jax.sharding import Mesh, PartitionSpec as P

HEADS = 8
MAPS = 16
HD = 128
VD = 256
KEYS = 256
DEVICES = 256
CHIPS = 128
PLANE = 16
COLUMN = 8
SUMS = MAPS * VD
WIDE = SUMS + 128
LINES = 40
LAG = 5
NEG = -1e30
AXES = ("x1", "x0", "z0", "y1", "y0", "z2", "z1", "core")
PLANE_AXES = ("x0", "x1", "y1", "y0")
COLUMN_AXES = ("z0", "z1", "z2")
BF16 = jnp.bfloat16
F32 = jnp.float32


def causal_mask(mask_ref):
    core = lax.axis_index("core")
    place = core
    row = lax.broadcasted_iota(jnp.int32, (CHIPS, 1), 0)
    device = row * 0 + core
    for bit, axis in enumerate(reversed(PLANE_AXES + COLUMN_AXES)):
        weight = 1 << (len(AXES) - 1 - AXES.index(axis))
        place += lax.axis_index(axis) * weight
        device += ((row >> bit) & 1) * weight
    last = device + (DEVICES - 1) * KEYS
    last_a = last - place * KEYS
    last_b = last - (place + 1 - 2 * core) * KEYS
    key = lax.broadcasted_iota(jnp.int32, (CHIPS, KEYS), 1)
    mask_ref[:, :KEYS] = jnp.where(key <= last_a, 0.0, NEG)
    mask_ref[:, KEYS:] = jnp.where(key <= last_b, 0.0, NEG)


def own_row(in_ref, mask_ref, out_ref):
    row = in_ref[...].astype(F32)
    tall = jnp.concatenate([row[:, start * HD : (start + 1) * HD] for start in range(MAPS)], axis=0)
    tall = tall.astype(BF16)
    for copy in range(COLUMN):
        out_ref[copy] = tall


def repeat_rows(in_ref, out_ref):
    rows = in_ref[...].astype(F32)
    wide = jnp.concatenate([rows[:, index, :] for index in range(MAPS)], axis=1)
    wide = jnp.concatenate([wide, wide], axis=0).astype(BF16)
    for start in range(0, CHIPS, 2 * COLUMN):
        out_ref[start : start + 2 * COLUMN, :] = wide


def attend(q_ref, ka_ref, kb_ref, va_ref, vb_ref, mask_ref, out_ref):
    lane = lax.broadcasted_iota(jnp.int32, (CHIPS, 128), 1)
    scaling = math.log2(math.e) / math.sqrt(HD)
    trans = (((1,), (1,)), ((), ()))
    stats = jnp.zeros((CHIPS, 128), F32)
    waiting = []
    for index in range(MAPS + LAG):
        if index < MAPS:
            cols = slice(index * HD, (index + 1) * HD)
            q = q_ref[:, cols]
            sa = lax.dot_general(q, ka_ref[:, cols], trans, preferred_element_type=F32) * scaling
            sb = lax.dot_general(q, kb_ref[:, cols], trans, preferred_element_type=F32) * scaling
            sa = sa + mask_ref[:, :KEYS]
            sb = sb + mask_ref[:, KEYS:]
            wide = jnp.maximum(sa, sb)
            wide = jnp.maximum(wide[:, :HD], wide[:, HD:]).astype(BF16)
            top = jnp.max(wide, axis=1, keepdims=True).astype(F32)
            ea = jnp.exp2(sa - top)
            eb = jnp.exp2(sb - top)
            total = jnp.sum(ea + eb, axis=1, keepdims=True)
            waiting.append((ea.astype(BF16), eb.astype(BF16)))
            stats = jnp.where(lane == index, top, stats)
            stats = jnp.where(lane == index + MAPS, total, stats)
        if index >= LAG:
            done = index - LAG
            cols = slice(done // 2 * VD, (done // 2 + 1) * VD)
            ea, eb = waiting[done]
            acc = jnp.dot(ea, va_ref[:, cols], preferred_element_type=F32)
            acc += jnp.dot(eb, vb_ref[:, cols], preferred_element_type=F32)
            out_ref[:, done * VD : (done + 1) * VD] = acc.astype(BF16)
    high = stats.astype(BF16).astype(F32)
    low = jnp.where(lane < 3 * MAPS, pltpu.roll(stats - high, MAPS, 1), 0.0)
    out_ref[:, SUMS:] = jnp.where(lane < 2 * MAPS, high, low).astype(BF16)


def merge_plane(in_ref, out_ref, lines_ref):
    stats = in_ref[:, SUMS:].astype(F32)
    total = pltpu.roll(stats, 128 - MAPS, 1) + pltpu.roll(stats, 128 - 2 * MAPS, 1)
    stats = stats.reshape(PLANE, COLUMN, 128)
    total = total.reshape(PLANE, COLUMN, 128)
    top = jnp.max(stats, axis=0)
    weight = jnp.exp2(stats - top[None])
    total = jnp.sum(weight * total, axis=0)
    lane = lax.broadcasted_iota(jnp.int32, (COLUMN, 128), 1)
    high = total.astype(BF16).astype(F32)
    low = jnp.where(lane < 3 * MAPS, pltpu.roll(total - high, 2 * MAPS, 1), 0.0)
    tail = jnp.where(lane < 2 * MAPS, pltpu.roll(high, MAPS, 1), low)
    lines_ref[pl.ds(2 * MAPS, COLUMN, stride=LINES), :] = jnp.where(lane < MAPS, top, tail)
    for line in range(2 * MAPS + 1, LINES):
        lines_ref[pl.ds(line, COLUMN, stride=LINES), :] = jnp.zeros((COLUMN, 128), F32)
    for line in range(2 * MAPS):
        part = in_ref[:, line * 128 : (line + 1) * 128].astype(F32).reshape(PLANE, COLUMN, 128)
        index = line // 2
        lines_ref[pl.ds(line, COLUMN, stride=LINES), :] = jnp.sum(
            part * weight[:, :, index : index + 1], axis=0
        )
    out_ref[...] = lines_ref[...].astype(BF16)


def merge_column(lam_ref, in_ref, gain_ref, out_ref, lines_ref):
    lines_ref[...] = in_ref[...].astype(F32)
    stats = lines_ref[pl.ds(2 * MAPS, COLUMN, stride=LINES), :]
    total = pltpu.roll(stats, 128 - MAPS, 1) + pltpu.roll(stats, 128 - 2 * MAPS, 1)
    top = jnp.max(stats, axis=0, keepdims=True)
    weight = jnp.exp2(stats - top)
    lane = lax.broadcasted_iota(jnp.int32, (COLUMN, 128), 1)
    total = jnp.where(lane < MAPS, jnp.sum(weight * total, axis=0, keepdims=True), 1.0)
    weight = weight / total
    for head in range(HEADS):
        one = weight[:, 2 * head : 2 * head + 1]
        two = weight[:, 2 * head + 1 : 2 * head + 2] * lam_ref[:, head : head + 1]
        halves = []
        for half in range(2):
            first = lines_ref[pl.ds(4 * head + half, COLUMN, stride=LINES), :] * one
            second = lines_ref[pl.ds(4 * head + 2 + half, COLUMN, stride=LINES), :] * two
            halves.append(jnp.sum(first - second, axis=0, keepdims=True))
        squares = halves[0] * halves[0] + halves[1] * halves[1]
        meansq = jnp.sum(squares, axis=1, keepdims=True) / VD
        factor = 1.0 / jnp.sqrt(meansq + 1e-5)
        for half in range(2):
            cols = slice(head * VD + half * 128, head * VD + half * 128 + 128)
            out_ref[:, cols] = (halves[half] * factor * gain_ref[:, cols]).astype(BF16)


def shards(queries, key_maps, values, lambdas, norm_gain):
    swap = [(0, 1), (1, 0)]
    key_other = lax.ppermute(key_maps, "core", swap)
    value_other = lax.ppermute(values, "core", swap)

    vmem = pl.BlockSpec(memory_space=pltpu.VMEM)
    mask = pl.pallas_call(
        causal_mask,
        out_specs=vmem,
        out_shape=jax.ShapeDtypeStruct((CHIPS, 2 * KEYS), F32),
        compiler_params=pltpu.CompilerParams(vmem_limit_bytes=8 << 20),
        cost_estimate=pl.CostEstimate(flops=1 << 31, bytes_accessed=1 << 18, transcendentals=0),
        name="causal_mask",
    )()
    spread = pl.pallas_call(
        own_row,
        in_specs=[vmem, vmem],
        out_specs=vmem,
        out_shape=jax.ShapeDtypeStruct((COLUMN, MAPS, HD), BF16),
        compiler_params=pltpu.CompilerParams(vmem_limit_bytes=8 << 20),
        name="own_row",
    )(queries, mask)
    column = lax.all_to_all(spread, COLUMN_AXES, 0, 0, tiled=True)
    spread = pl.pallas_call(
        repeat_rows,
        in_specs=[vmem],
        out_specs=vmem,
        out_shape=jax.ShapeDtypeStruct((CHIPS, MAPS * HD), BF16),
        compiler_params=pltpu.CompilerParams(vmem_limit_bytes=8 << 20),
        cost_estimate=pl.CostEstimate(flops=1 << 31, bytes_accessed=1 << 20, transcendentals=0),
        name="repeat_rows",
    )(column)
    spread = spread.reshape(PLANE, COLUMN, MAPS * HD)
    q_all = lax.all_to_all(spread, PLANE_AXES, 0, 0, tiled=True).reshape(CHIPS, MAPS * HD)

    partial = pl.pallas_call(
        attend,
        in_specs=[vmem] * 6,
        out_specs=vmem,
        out_shape=jax.ShapeDtypeStruct((CHIPS, WIDE), BF16),
        compiler_params=pltpu.CompilerParams(vmem_limit_bytes=16 << 20),
        name="attend",
    )(q_all, key_maps, key_other, values, value_other, mask)

    partial = partial.reshape(PLANE, COLUMN, WIDE)
    partial = lax.all_to_all(partial, PLANE_AXES, 0, 0, tiled=True)
    merged = pl.pallas_call(
        merge_plane,
        in_specs=[vmem],
        out_specs=vmem,
        out_shape=jax.ShapeDtypeStruct((COLUMN * LINES, 128), BF16),
        scratch_shapes=[pltpu.VMEM((COLUMN * LINES, 128), F32)],
        compiler_params=pltpu.CompilerParams(vmem_limit_bytes=8 << 20),
        name="merge_plane",
    )(partial.reshape(CHIPS, WIDE))
    merged = merged.reshape(COLUMN, LINES, 128)
    merged = lax.all_to_all(merged, COLUMN_AXES, 0, 0, tiled=True)
    return pl.pallas_call(
        merge_column,
        in_specs=[vmem, vmem, vmem],
        out_specs=vmem,
        out_shape=jax.ShapeDtypeStruct((1, HEADS * VD), BF16),
        scratch_shapes=[pltpu.VMEM((COLUMN * LINES, 128), F32)],
        compiler_params=pltpu.CompilerParams(vmem_limit_bytes=8 << 20),
        name="merge_column",
    )(lambdas.reshape(1, HEADS), merged.reshape(COLUMN * LINES, 128), norm_gain.reshape(1, HEADS * VD))


def solution(mesh):
    fine = Mesh(mesh.devices.reshape((2,) * len(AXES)), AXES)
    rows = P(AXES, None)
    return jax.shard_map(
        shards,
        mesh=fine,
        in_specs=(rows, rows, rows, P(), P()),
        out_specs=rows,
        check_vma=False,
    )
```
